1024 devices in a mesh: group: 4 (over y_hi), blk: 256 (over z, y_lo, x, core).
Axes of the slice: x: 8, y: 8 (y_hi: 4, y_lo: 2; y = y_hi * 2 + y_lo), z: 8, core: 2. Of those that a mesh axis runs over, the one named last changes fastest.
Arguments:
- image_emb: bfloat16 [262144, 1152], P(('group', 'blk')), may hold values from -4 to 4
- text_emb: bfloat16 [262144, 1152], P(('group', 'blk')), may hold values from -4 to 4
- image_ids: int32 [262144], P(('group', 'blk')), may hold values from 0 to 127
- text_ids: int32 [262144], P(('group', 'blk')), may hold values from 0 to 127
Outputs:
- row_loss: float32 [262144], P(('group', 'blk'))
- image_grad: bfloat16 [262144, 1152], P(('group', 'blk'))
- text_grad: bfloat16 [262144, 1152], P(('group', 'blk'))
The draws below stay inside these ranges and needn't reach their ends.
All inputs are finite; a program needn't handle non-finite values.
Results may differ from the reference program's by a relative error of at most 0.0077.
Values may be sent and summed in bfloat16 or wider, within the bound.
A program may use at most 32 MiB of HBM per device.

```python
import math
import jax
import jax.numpy as jnp

D = 1152
TOK_DEV = 256
PAIR_IDS = 128
TOKENS = 262144
N_GROUP = 4
N_BLK = 256


def spread_rows(noise, scale_key, low, high):
    scales = jnp.exp(jax.random.uniform(scale_key, (TOKENS, 1), jnp.float32, math.log(low), math.log(high)))
    return scales * noise / math.sqrt(D)


def draw_image_emb(key, part):
    key = jax.random.fold_in(key, 11)
    noise_key, scale_key = jax.random.split(key)
    noise = jnp.clip(jax.random.normal(noise_key, (TOKENS, D), jnp.float32), -5.0, 5.0)
    rows = spread_rows(noise, scale_key, 0.6, 6.0)
    return rows.astype(jnp.bfloat16)


def draw_text_emb(key, part):
    key = jax.random.fold_in(key, 12)
    noise_key, scale_key = jax.random.split(key)
    noise = jnp.clip(jax.random.normal(noise_key, (TOKENS, D), jnp.float32), -5.0, 5.0)
    rows = spread_rows(noise, scale_key, 0.6, 6.0)
    return rows.astype(jnp.bfloat16)


def place_ends(array, key, smallest, top_value):
    longest = array.shape.index(max(array.shape))
    spots = []
    for shift in (0, 1):
        where = [jax.random.randint(jax.random.fold_in(key, axis), (), 0, length) for axis, length in enumerate(array.shape)]
        where[longest] = (where[longest] + shift) % array.shape[longest]
        spots.append(tuple(where))
    return array.at[spots[0]].set(smallest).at[spots[1]].set(top_value)


def setup_inputs(seed: int = 0) -> dict:
    keys = jax.random.split(jax.random.key(seed), 5)
    image_emb = draw_image_emb(jax.random.fold_in(keys[4], 71), 0)
    text_emb = draw_text_emb(jax.random.fold_in(keys[4], 71), 0)
    image_ids = place_ends(jax.random.randint(keys[2], (TOKENS,), 0, PAIR_IDS), jax.random.fold_in(keys[2], 1), 0, PAIR_IDS - 1).astype(jnp.int32)
    text_ids = place_ends(jax.random.randint(keys[3], (TOKENS,), 0, PAIR_IDS), jax.random.fold_in(keys[3], 1), 0, PAIR_IDS - 1).astype(jnp.int32)
    return dict(image_emb=image_emb, text_emb=text_emb, image_ids=image_ids, text_ids=text_ids)


logit_scale = 10.0
logit_bias = -3.0


def reference(image_emb, text_emb, image_ids, text_ids):
    shape = (N_GROUP, N_BLK, TOK_DEV, D)
    images = image_emb.reshape(shape).astype(jnp.float32)
    texts = text_emb.reshape(shape).astype(jnp.float32)
    img_tags = image_ids.reshape(N_GROUP, N_BLK, TOK_DEV)
    txt_tags = text_ids.reshape(N_GROUP, N_BLK, TOK_DEV)
    visits = [(0, 0), (1, 1), (2, 1), (1, 0)]
    loss_total = jnp.zeros((N_GROUP, N_BLK, TOK_DEV), jnp.float32)
    image_total = jnp.zeros(shape, jnp.float32)
    text_total = jnp.zeros(shape, jnp.float32)
    for amount, axis in visits:
        block = jnp.roll(texts, amount, axis=axis)
        tags = jnp.roll(txt_tags, amount, axis=axis)
        scores = jnp.einsum("gbrd,gbsd->gbrs", images, block)
        logits = logit_scale * scores + logit_bias
        pair_sign = jnp.where(img_tags[..., :, None] == tags[..., None, :], 1.0, -1.0).astype(jnp.float32)
        loss_total = loss_total + jnp.sum(jax.nn.softplus(-pair_sign * logits), axis=-1)
        slopes = (-pair_sign * jax.nn.sigmoid(-pair_sign * logits)).astype(jnp.bfloat16).astype(jnp.float32)
        image_total = image_total + logit_scale * jnp.einsum("gbrs,gbsd->gbrd", slopes, block)
        text_part = logit_scale * jnp.einsum("gbrs,gbrd->gbsd", slopes, images)
        text_total = text_total + jnp.roll(text_part, -amount, axis=axis)
    row_loss = (loss_total / (4 * TOK_DEV)).reshape(TOKENS)
    image_grad = image_total.reshape(TOKENS, D).astype(jnp.bfloat16)
    text_grad = text_total.reshape(TOKENS, D).astype(jnp.bfloat16)
    return row_loss, image_grad, text_grad
```

```python
import functools

import jax
import jax.numpy as jnp
from jax import lax
from jax.experimental import pallas as pl
from jax.experimental.pallas import tpu as pltpu
from jax.sharding import PartitionSpec as P

logit_scale = 10.0
logit_bias = -3.0
MESH = pl.DeviceIdType.MESH
CHUNK = 128

OWN_T, OWN_I, FAR_T, FAR_I, NEAR_T, NEAR_I, CROSS_T, CROSS_I = range(8)


def kernel(n_group, n_blk, image, text, image_ids, text_ids, loss, image_grad, text_grad,
           slots, tags, column_tags, acc, loss_acc, send, recv, tag_send, tag_recv):
    g, b = lax.axis_index("group"), lax.axis_index("blk")
    rows = image.shape[0]
    chunks = rows // CHUNK
    core = lax.rem(b, 2)
    partner = (g, b + 1 - 2 * core)
    ahead, behind = (g, lax.rem(b + 2, n_blk)), (g, lax.rem(b + n_blk - 2, n_blk))
    above, below = (lax.rem(g + 1, n_group), b), (lax.rem(g + n_group - 1, n_group), b)

    barrier = pltpu.get_barrier_semaphore()
    others = (partner, ahead, behind, above, below)
    for other in others:
        pl.semaphore_signal(barrier, inc=1, device_id=other, device_id_type=MESH)

    def span(k):
        return pl.ds(k * CHUNK, CHUNK)

    def local(source, slot, k):
        return pltpu.make_async_copy(source.at[span(k)], slots.at[slot, span(k)], recv.at[slot, k])

    def remote(source, slot, k, device):
        return pltpu.make_async_remote_copy(
            source.at[span(k)], slots.at[slot, span(k)], send.at[slot, k], recv.at[slot, k],
            device_id=device, device_id_type=MESH)

    def remote_tag(source, slot, device):
        return pltpu.make_async_remote_copy(
            source, tags.at[slot], tag_send.at[slot], tag_recv.at[slot],
            device_id=device, device_id_type=MESH)

    for slot, source, ids in ((OWN_T, text, text_ids), (OWN_I, image, image_ids)):
        for k in range(chunks):
            local(source, slot, k).start()
        tags[slot] = ids[...]
    for side, ids in ((0, image_ids), (1, text_ids)):
        column_tags[side] = jnp.transpose(jnp.broadcast_to(ids[...], (CHUNK, rows)))
    acc[...] = jnp.zeros_like(acc)
    loss_acc[...] = jnp.zeros_like(loss_acc)
    pl.semaphore_wait(barrier, len(others))

    plan = ((FAR_T, text, text_ids, ahead), (FAR_I, image, image_ids, behind),
            (CROSS_T, text, text_ids, above), (CROSS_I, image, image_ids, below))
    for slot, source, ids, device in plan:
        remote_tag(ids, slot, device).start()
    for slot, source, ids, device in plan:
        for k in range(chunks):
            remote(source, slot, k, device).start()

    @pl.when(core == 0)
    def _():
        remote_tag(text_ids, NEAR_T, partner).start()
        for k in range(chunks):
            remote(text, NEAR_T, k, partner).start()

    @pl.when(core == 1)
    def _():
        remote_tag(image_ids, NEAR_I, partner).start()
        for k in range(chunks):
            remote(image, NEAR_I, k, partner).start()

    def score(side, slot, k):
        mine = slots[OWN_I if side == 0 else OWN_T]
        theirs = slots[slot, span(k)]
        scores = lax.dot_general(mine, theirs, (((1,), (1,)), ((), ())), preferred_element_type=jnp.float32)
        logits = logit_scale * scores + logit_bias
        matched = column_tags[side] == tags[slot, :, span(k)]
        signed = jnp.where(matched, -logits, logits)
        small = jnp.exp(-jnp.abs(signed))
        sigmoid = jnp.where(signed >= 0, 1.0, small) / (1.0 + small)
        if side == 0:
            loss_acc[...] += jnp.maximum(signed, 0.0) + jnp.log1p(small)
        slopes = jnp.where(matched, -sigmoid, sigmoid).astype(jnp.bfloat16)
        acc[side] += jnp.dot(slopes, theirs, preferred_element_type=jnp.float32)

    for k in range(chunks):
        local(text, OWN_T, k).wait()
        local(image, OWN_I, k).wait()
    for side, slot in ((0, OWN_T), (1, OWN_I)):
        for k in range(chunks):
            score(side, slot, k)
    remote_tag(text_ids, FAR_T, ahead).wait_recv()
    remote_tag(image_ids, FAR_I, behind).wait_recv()

    @pl.when(core == 0)
    def _():
        remote_tag(tags.at[FAR_I], NEAR_I, partner).start()

    @pl.when(core == 1)
    def _():
        remote_tag(tags.at[FAR_T], NEAR_T, partner).start()

    for k in range(chunks):
        for side, slot, source, device in ((0, FAR_T, text, ahead), (1, FAR_I, image, behind)):
            remote(source, slot, k, device).wait_recv()

            @pl.when(core == 1 - side)
            def _(side=side, slot=slot, k=k):
                remote(slots.at[slot], NEAR_T if side == 0 else NEAR_I, k, partner).start()

            score(side, slot, k)
    remote_tag(text_ids, NEAR_T, partner).wait_recv()
    remote_tag(image_ids, NEAR_I, partner).wait_recv()
    for k in range(chunks):
        for side, slot, source in ((0, NEAR_T, text), (1, NEAR_I, image)):
            remote(source, slot, k, partner).wait_recv()
            score(side, slot, k)
    remote_tag(text_ids, CROSS_T, above).wait_recv()
    remote_tag(image_ids, CROSS_I, below).wait_recv()
    for k in range(chunks):
        for side, slot, source, device in ((0, CROSS_T, text, above), (1, CROSS_I, image, below)):
            remote(source, slot, k, device).wait_recv()
            score(side, slot, k)

    image_grad[...] = (logit_scale * acc[0]).astype(image_grad.dtype)
    text_grad[...] = (logit_scale * acc[1]).astype(text_grad.dtype)
    total = jnp.sum(jnp.transpose(loss_acc[...]), axis=0, keepdims=True)
    loss[...] = total / (4 * rows)

    for slot, source, ids, device in plan + ((NEAR_T, text, text_ids, partner), (NEAR_I, image, image_ids, partner)):
        remote_tag(ids, slot, device).wait_send()
        for k in range(chunks):
            remote(source, slot, k, device).wait_send()


def per_device(n_group, n_blk, image_emb, text_emb, image_ids, text_ids):
    rows, width = image_emb.shape
    chunks = rows // CHUNK
    in_vmem = pl.BlockSpec(memory_space=pltpu.VMEM)
    in_place = pl.BlockSpec(memory_space=pl.ANY)
    loss, image_grad, text_grad = pl.pallas_call(
        functools.partial(kernel, n_group, n_blk),
        out_shape=(
            jax.ShapeDtypeStruct((1, rows), jnp.float32),
            jax.ShapeDtypeStruct((rows, width), jnp.bfloat16),
            jax.ShapeDtypeStruct((rows, width), jnp.bfloat16),
        ),
        in_specs=[in_place, in_place, in_vmem, in_vmem],
        out_specs=(in_vmem, in_vmem, in_vmem),
        scratch_shapes=[
            pltpu.VMEM((8, rows, width), jnp.bfloat16),
            pltpu.VMEM((8, 1, rows), jnp.int32),
            pltpu.VMEM((2, rows, CHUNK), jnp.int32),
            pltpu.VMEM((2, rows, width), jnp.float32),
            pltpu.VMEM((rows, CHUNK), jnp.float32),
            pltpu.SemaphoreType.DMA((8, chunks)),
            pltpu.SemaphoreType.DMA((8, chunks)),
            pltpu.SemaphoreType.DMA((8,)),
            pltpu.SemaphoreType.DMA((8,)),
        ],
        compiler_params=pltpu.CompilerParams(collective_id=0, has_side_effects=True, vmem_limit_bytes=60 * 2**20),
        cost_estimate=pl.CostEstimate(flops=2 * 16 * rows * rows * width, bytes_accessed=8 * rows * width, transcendentals=0),
    )(image_emb, text_emb, image_ids.reshape(1, rows), text_ids.reshape(1, rows))
    return loss.reshape(rows), image_grad, text_grad


def solution(mesh):
    sizes = dict(mesh.shape)
    vector, matrix = P(("group", "blk")), P(("group", "blk"), None)
    return jax.shard_map(
        functools.partial(per_device, sizes["group"], sizes["blk"]), mesh=mesh,
        in_specs=(matrix, matrix, vector, vector), out_specs=(vector, matrix, matrix), check_vma=False)
```

```python
import functools

import jax
import jax.numpy as jnp
from jax import lax
from jax.experimental import pallas as pl
from jax.experimental.pallas import tpu as pltpu
from jax.sharding import PartitionSpec as P

logit_scale = 10.0
logit_bias = -3.0
MESH = pl.DeviceIdType.MESH
CHUNK = 128
COLUMNS = 8
PIECES = 4

OWN_T, OWN_I, FAR_T, FAR_I, NEAR_T, NEAR_I, CROSS_T, CROSS_I = range(8)
A_PARTNER, A_AHEAD, A_BEHIND, A_ABOVE, A_BELOW, A_DEST_T, A_DEST_I = range(7)


def kernel(n_group, n_blk, image, text, image_ids, text_ids, loss, image_grad, text_grad,
           slots, relay, tags, column_tags, acc, loss_acc,
           send, recv, tag_send, tag_recv, relay_send, relay_recv, answer, answer_t, answer_i):
    g, b = lax.axis_index("group"), lax.axis_index("blk")
    rows = image.shape[0]
    chunks = rows // CHUNK
    part = rows // COLUMNS
    per_chunk = CHUNK // part
    depth = n_blk // (4 * COLUMNS)
    core, x = lax.rem(b, 2), lax.rem(b // 2, COLUMNS)
    low_y, z = lax.rem(b // (2 * COLUMNS), 2), b // (4 * COLUMNS)
    last = COLUMNS - 1

    def at(z_, y_, x_):
        return (g, z_ * (4 * COLUMNS) + y_ * (2 * COLUMNS) + x_ * 2 + core)

    partner = (g, b + 1 - 2 * core)
    ahead, behind = (g, lax.rem(b + 2, n_blk)), (g, lax.rem(b + n_blk - 2, n_blk))
    above, below = (lax.rem(g + 1, n_group), b), (lax.rem(g + n_group - 1, n_group), b)

    def crossing(k):
        return at(z, 1 - low_y, k)

    source_t, source_i = at(z, 1 - low_y, last), at(z, 1 - low_y, 0)
    dest_t = at(lax.rem(z + 1 - low_y, depth), low_y, 0)
    dest_i = at(lax.rem(z + depth - low_y, depth), low_y, last)

    def relay_t(k):
        return at(lax.rem(z + depth - 1 + low_y, depth), low_y, k)

    def relay_i(k):
        return at(lax.rem(z + low_y, depth), low_y, k)

    def order(device):
        index = device[0] * n_blk + device[1]
        return jnp.where(index == 0, n_group * n_blk, index)

    me = order((g, b))

    def lower(device):
        return order(device) < me

    first, final = x == 0, x == last
    barrier = pltpu.get_barrier_semaphore()

    def announce(device, when=True):
        @pl.when(jnp.logical_and(when, me < order(device)))
        def _():
            pl.semaphore_signal(barrier, inc=1, device_id=device, device_id_type=MESH)

    def reply(device, semaphore, when=True):
        @pl.when(jnp.logical_and(when, lower(device)))
        def _():
            pl.semaphore_signal(semaphore, inc=1, device_id=device, device_id_type=MESH)

    def hear(device, semaphore, when=True):
        @pl.when(jnp.logical_and(when, me < order(device)))
        def _():
            pl.semaphore_wait(semaphore, 1)

    count = jnp.int32(0)
    for device, when in ((partner, True), (ahead, True), (behind, True), (above, True), (below, True),
                         (source_t, x > 0), (source_i, x < last), (dest_t, x > 0), (dest_i, x < last)):
        announce(device, when)
        count += jnp.where(jnp.logical_and(when, lower(device)), 1, 0)
    for k in range(COLUMNS):
        for device, when in ((crossing(k), final if k > 0 else None), (crossing(k), first if k < last else None),
                             (relay_t(k), first if k > 0 else None), (relay_i(k), final if k < last else None)):
            if when is not None:
                announce(device, when)
                count += jnp.where(jnp.logical_and(when, lower(device)), 1, 0)

    def span(k):
        return pl.ds(k * CHUNK, CHUNK)

    def local(source, slot, k):
        return pltpu.make_async_copy(source.at[span(k)], slots.at[slot, span(k)], recv.at[slot, k])

    def remote(source, slot, k, device):
        return pltpu.make_async_remote_copy(
            source.at[span(k)], slots.at[slot, span(k)], send.at[slot, k], recv.at[slot, k],
            device_id=device, device_id_type=MESH)

    def remote_tag(source, slot, device):
        return pltpu.make_async_remote_copy(
            source, tags.at[slot], tag_send.at[slot], tag_recv.at[slot],
            device_id=device, device_id_type=MESH)

    def direct_part(source, slot, k, device):
        return pltpu.make_async_remote_copy(
            source.at[pl.ds(k * part, part)], slots.at[slot, pl.ds(k * part, part)],
            send.at[slot, k // per_chunk], recv.at[slot, k // per_chunk],
            device_id=device, device_id_type=MESH)

    def to_relay(source, side, k, device):
        return pltpu.make_async_remote_copy(
            source.at[pl.ds(k * part, part)], relay.at[side],
            send.at[FAR_T + side, k // per_chunk], relay_recv.at[side],
            device_id=device, device_id_type=MESH)

    def from_relay(side, device):
        return pltpu.make_async_remote_copy(
            relay.at[side], slots.at[FAR_T + side, pl.ds(pl.multiple_of(x * part, part), part)],
            relay_send.at[side], recv.at[FAR_T + side, x // per_chunk],
            device_id=device, device_id_type=MESH)

    for slot, source, ids in ((OWN_T, text, text_ids), (OWN_I, image, image_ids)):
        for k in range(chunks):
            local(source, slot, k).start()
        tags[slot] = ids[...]
    for side, ids in ((0, image_ids), (1, text_ids)):
        column_tags[side] = jnp.transpose(jnp.broadcast_to(ids[...], (CHUNK, rows)))
    acc[...] = jnp.zeros_like(acc)
    loss_acc[...] = jnp.zeros_like(loss_acc)

    @pl.when(count > 0)
    def _():
        pl.semaphore_wait(barrier, count)

    reply(partner, answer.at[A_PARTNER])
    reply(ahead, answer.at[A_BEHIND])
    reply(behind, answer.at[A_AHEAD])
    reply(above, answer.at[A_BELOW])
    reply(below, answer.at[A_ABOVE])
    reply(source_t, answer_t.at[x], x > 0)
    reply(source_i, answer_i.at[x], x < last)
    for k in range(COLUMNS):
        if k > 0:
            reply(relay_t(k), answer.at[A_DEST_T], first)
        if k < last:
            reply(relay_i(k), answer.at[A_DEST_I], final)

    hear(partner, answer.at[A_PARTNER])

    @pl.when(core == 0)
    def _():
        remote_tag(text_ids, NEAR_T, partner).start()
        for k in range(chunks):
            remote(text, NEAR_T, k, partner).start()

    @pl.when(core == 1)
    def _():
        remote_tag(image_ids, NEAR_I, partner).start()
        for k in range(chunks):
            remote(image, NEAR_I, k, partner).start()

    @pl.when(final)
    def _():
        for k in range(1, COLUMNS):
            hear(crossing(k), answer_t.at[k])
            to_relay(text, 0, k, crossing(k)).start()

    @pl.when(first)
    def _():
        for k in range(COLUMNS - 1):
            hear(crossing(k), answer_i.at[k])
            to_relay(image, 1, k, crossing(k)).start()

    hear(above, answer.at[A_ABOVE])
    remote_tag(text_ids, CROSS_T, above).start()
    for k in range(chunks):
        remote(text, CROSS_T, k, above).start()
    hear(below, answer.at[A_BELOW])
    remote_tag(image_ids, CROSS_I, below).start()
    for k in range(chunks):
        remote(image, CROSS_I, k, below).start()

    hear(ahead, answer.at[A_AHEAD])
    remote_tag(text_ids, FAR_T, ahead).start()

    @pl.when(final)
    def _():
        direct_part(text, FAR_T, 0, ahead).start()

    @pl.when(jnp.logical_not(final))
    def _():
        for k in range(chunks):
            remote(text, FAR_T, k, ahead).start()

    def send_behind():
        hear(behind, answer.at[A_BEHIND])
        remote_tag(image_ids, FAR_I, behind).start()

        @pl.when(first)
        def _():
            direct_part(image, FAR_I, last, behind).start()

        @pl.when(jnp.logical_not(first))
        def _():
            for k in range(chunks):
                remote(image, FAR_I, k, behind).start()

    def pass_on(side):
        pltpu.make_async_copy(relay.at[side], relay.at[side], relay_recv.at[side]).wait()
        device = dest_t if side == 0 else dest_i
        hear(device, answer.at[A_DEST_T + side])
        from_relay(side, device).start()

    def score(side, slot, k):
        mine = slots[OWN_I if side == 0 else OWN_T]
        theirs = slots[slot, span(k)]
        scores = lax.dot_general(mine, theirs, (((1,), (1,)), ((), ())), preferred_element_type=jnp.float32)
        logits = logit_scale * scores + logit_bias
        matched = column_tags[side] == tags[slot, :, span(k)]
        signed = jnp.where(matched, -logits, logits)
        small = jnp.exp(-jnp.abs(signed))
        sigmoid = jnp.where(signed >= 0, 1.0, small) / (1.0 + small)
        if side == 0:
            loss_acc[...] += jnp.maximum(signed, 0.0) + jnp.log1p(small)
        slopes = jnp.where(matched, -sigmoid, sigmoid).astype(jnp.bfloat16)
        acc[side] += jnp.dot(slopes, theirs, preferred_element_type=jnp.float32)

    late = b < 2
    late_relay = jnp.logical_and(z == 0, low_y == 1)

    @pl.when(jnp.logical_not(late))
    def _():
        send_behind()

    for k in range(chunks):
        local(text, OWN_T, k).wait()
        local(image, OWN_I, k).wait()
    for side, slot in ((0, OWN_T), (1, OWN_I)):
        for k in range(chunks):
            score(side, slot, k)

    @pl.when(x > 0)
    def _():
        pass_on(0)

    @pl.when(jnp.logical_and(x < last, jnp.logical_not(late_relay)))
    def _():
        pass_on(1)

    @pl.when(late)
    def _():
        send_behind()

    remote_tag(text_ids, FAR_T, ahead).wait_recv()
    remote_tag(image_ids, FAR_I, behind).wait_recv()

    @pl.when(core == 0)
    def _():
        remote_tag(tags.at[FAR_I], NEAR_I, partner).start()

    @pl.when(core == 1)
    def _():
        remote_tag(tags.at[FAR_T], NEAR_T, partner).start()

    for k in range(chunks):
        for side, slot, source, device in ((0, FAR_T, text, ahead), (1, FAR_I, image, behind)):
            remote(source, slot, k, device).wait_recv()

            @pl.when(core == 1 - side)
            def _(side=side, slot=slot, k=k):
                remote(slots.at[slot], NEAR_T if side == 0 else NEAR_I, k, partner).start()

            score(side, slot, k)

    @pl.when(jnp.logical_and(x < last, late_relay))
    def _():
        pass_on(1)

    remote_tag(text_ids, NEAR_T, partner).wait_recv()
    remote_tag(image_ids, NEAR_I, partner).wait_recv()
    for k in range(chunks):
        for side, slot, source in ((0, NEAR_T, text), (1, NEAR_I, image)):
            remote(source, slot, k, partner).wait_recv()
            score(side, slot, k)
    remote_tag(text_ids, CROSS_T, above).wait_recv()
    remote_tag(image_ids, CROSS_I, below).wait_recv()
    for k in range(chunks):
        for side, slot, source, device in ((0, CROSS_T, text, above), (1, CROSS_I, image, below)):
            remote(source, slot, k, device).wait_recv()
            score(side, slot, k)

    image_grad[...] = (logit_scale * acc[0]).astype(image_grad.dtype)
    text_grad[...] = (logit_scale * acc[1]).astype(text_grad.dtype)
    total = jnp.sum(jnp.transpose(loss_acc[...]), axis=0, keepdims=True)
    loss[...] = total / (4 * rows)

    for slot, source, ids, device in (
            (FAR_T, text, text_ids, ahead), (FAR_I, image, image_ids, behind),
            (CROSS_T, text, text_ids, above), (CROSS_I, image, image_ids, below),
            (NEAR_T, text, text_ids, partner), (NEAR_I, image, image_ids, partner)):
        remote_tag(ids, slot, device).wait_send()
        for k in range(chunks):
            remote(source, slot, k, device).wait_send()

    @pl.when(x > 0)
    def _():
        from_relay(0, dest_t).wait_send()

    @pl.when(x < last)
    def _():
        from_relay(1, dest_i).wait_send()


def write_out(loss, image_grad, text_grad, loss_out, image_out, text_out, done):
    piece = image_grad.shape[0] // PIECES
    copies = [pltpu.make_async_copy(loss, loss_out, done.at[2 * PIECES])]
    for i, (source, target) in enumerate(((image_grad, image_out), (text_grad, text_out))):
        for k in range(PIECES):
            part = pl.ds(k * piece, piece)
            copies.append(pltpu.make_async_copy(source.at[part], target.at[part], done.at[i * PIECES + k]))
    for copy in copies:
        copy.start()
    for copy in copies:
        copy.wait()


def per_device(n_group, n_blk, image_emb, text_emb, image_ids, text_ids):
    rows, width = image_emb.shape
    chunks = rows // CHUNK
    in_vmem = pl.BlockSpec(memory_space=pltpu.VMEM)
    in_hbm = pl.BlockSpec(memory_space=pltpu.HBM)
    shapes = ((1, rows), jnp.float32), ((rows, width), jnp.bfloat16), ((rows, width), jnp.bfloat16)
    results = pl.pallas_call(
        functools.partial(kernel, n_group, n_blk),
        out_shape=tuple(pltpu.VMEM(*s) for s in shapes),
        in_specs=[in_hbm, in_hbm, in_vmem, in_vmem],
        out_specs=(in_vmem, in_vmem, in_vmem),
        scratch_shapes=[
            pltpu.VMEM((8, rows, width), jnp.bfloat16),
            pltpu.VMEM((2, rows // COLUMNS, width), jnp.bfloat16),
            pltpu.VMEM((8, 1, rows), jnp.int32),
            pltpu.VMEM((2, rows, CHUNK), jnp.int32),
            pltpu.VMEM((2, rows, width), jnp.float32),
            pltpu.VMEM((rows, CHUNK), jnp.float32),
            pltpu.SemaphoreType.DMA((8, chunks)),
            pltpu.SemaphoreType.DMA((8, chunks)),
            pltpu.SemaphoreType.DMA((8,)),
            pltpu.SemaphoreType.DMA((8,)),
            pltpu.SemaphoreType.DMA((2,)),
            pltpu.SemaphoreType.DMA((2,)),
            pltpu.SemaphoreType.REGULAR((7,)),
            pltpu.SemaphoreType.REGULAR((COLUMNS,)),
            pltpu.SemaphoreType.REGULAR((COLUMNS,)),
        ],
        compiler_params=pltpu.CompilerParams(collective_id=0, has_side_effects=True, vmem_limit_bytes=56 * 2**20),
        cost_estimate=pl.CostEstimate(flops=2 * 16 * rows * rows * width, bytes_accessed=8 * rows * width, transcendentals=0),
    )(image_emb, text_emb, image_ids.reshape(1, rows), text_ids.reshape(1, rows))
    loss, image_grad, text_grad = pl.pallas_call(
        write_out,
        out_shape=tuple(jax.ShapeDtypeStruct(*s) for s in shapes),
        in_specs=[in_vmem] * 3,
        out_specs=(in_hbm, in_hbm, in_hbm),
        scratch_shapes=[pltpu.SemaphoreType.DMA((2 * PIECES + 1,))],
        compiler_params=pltpu.CompilerParams(vmem_limit_bytes=4 * 2**20),
    )(*results)
    return loss.reshape(rows), image_grad, text_grad


def solution(mesh):
    sizes = dict(mesh.shape)
    vector, matrix = P(("group", "blk")), P(("group", "blk"), None)
    return jax.shard_map(
        functools.partial(per_device, sizes["group"], sizes["blk"]), mesh=mesh,
        in_specs=(matrix, matrix, vector, vector), out_specs=(vector, matrix, matrix), check_vma=False)
```

```python
import functools

import jax
import jax.numpy as jnp
from jax import lax
from jax.experimental import pallas as pl
from jax.experimental.pallas import tpu as pltpu
from jax.sharding import PartitionSpec as P

logit_scale = 10.0
logit_bias = -3.0
MESH = pl.DeviceIdType.MESH
CHUNK = 128
COLUMNS = 8
PIECES = 4

OWN_T, OWN_I, FAR_T, FAR_I, NEAR_T, NEAR_I, CROSS_T, CROSS_I = range(8)
A_PARTNER, A_AHEAD, A_BEHIND, A_ABOVE, A_BELOW, A_DEST_T, A_DEST_I = range(7)


def kernel(n_group, n_blk, image, text, image_ids, text_ids, loss, image_grad, text_grad,
           slots, relay, tags, column_tags, acc, loss_acc,
           send, recv, tag_send, tag_recv, relay_send, relay_recv, answer, answer_t, answer_i):
    g, b = lax.axis_index("group"), lax.axis_index("blk")
    rows = image.shape[0]
    chunks = rows // CHUNK
    part = rows // COLUMNS
    per_chunk = CHUNK // part
    depth = n_blk // (4 * COLUMNS)
    core, x = lax.rem(b, 2), lax.rem(b // 2, COLUMNS)
    low_y, z = lax.rem(b // (2 * COLUMNS), 2), b // (4 * COLUMNS)
    last = COLUMNS - 1

    def at(z_, y_, x_):
        return (g, z_ * (4 * COLUMNS) + y_ * (2 * COLUMNS) + x_ * 2 + core)

    partner = (g, b + 1 - 2 * core)
    ahead, behind = (g, lax.rem(b + 2, n_blk)), (g, lax.rem(b + n_blk - 2, n_blk))
    above, below = (lax.rem(g + 1, n_group), b), (lax.rem(g + n_group - 1, n_group), b)

    def crossing(k):
        return at(z, 1 - low_y, k)

    source_t, source_i = at(z, 1 - low_y, last), at(z, 1 - low_y, 0)
    dest_t = at(lax.rem(z + 1 - low_y, depth), low_y, 0)
    dest_i = at(lax.rem(z + depth - low_y, depth), low_y, last)

    def relay_t(k):
        return at(lax.rem(z + depth - 1 + low_y, depth), low_y, k)

    def relay_i(k):
        return at(lax.rem(z + low_y, depth), low_y, k)

    def order(device):
        index = device[0] * n_blk + device[1]
        return jnp.where(index == 0, n_group * n_blk, index)

    me = order((g, b))

    def lower(device):
        return order(device) < me

    first, final = x == 0, x == last
    barrier = pltpu.get_barrier_semaphore()

    def announce(device, when=True):
        @pl.when(jnp.logical_and(when, me < order(device)))
        def _():
            pl.semaphore_signal(barrier, inc=1, device_id=device, device_id_type=MESH)

    def reply(device, semaphore, when=True):
        @pl.when(jnp.logical_and(when, lower(device)))
        def _():
            pl.semaphore_signal(semaphore, inc=1, device_id=device, device_id_type=MESH)

    def hear(device, semaphore, when=True):
        @pl.when(jnp.logical_and(when, me < order(device)))
        def _():
            pl.semaphore_wait(semaphore, 1)

    count = jnp.int32(0)
    for device, when in ((partner, True), (ahead, True), (behind, True), (above, True), (below, True),
                         (source_t, x > 0), (source_i, x < last), (dest_t, x > 0), (dest_i, x < last)):
        announce(device, when)
        count += jnp.where(jnp.logical_and(when, lower(device)), 1, 0)
    for k in range(COLUMNS):
        for device, when in ((crossing(k), final if k > 0 else None), (crossing(k), first if k < last else None),
                             (relay_t(k), first if k > 0 else None), (relay_i(k), final if k < last else None)):
            if when is not None:
                announce(device, when)
                count += jnp.where(jnp.logical_and(when, lower(device)), 1, 0)

    def span(k):
        return pl.ds(k * CHUNK, CHUNK)

    def local(source, slot, k):
        return pltpu.make_async_copy(source.at[span(k)], slots.at[slot, span(k)], recv.at[slot, k])

    def remote(source, slot, k, device):
        return pltpu.make_async_remote_copy(
            source.at[span(k)], slots.at[slot, span(k)], send.at[slot, k], recv.at[slot, k],
            device_id=device, device_id_type=MESH)

    def remote_tag(source, slot, device):
        return pltpu.make_async_remote_copy(
            source, tags.at[slot], tag_send.at[slot], tag_recv.at[slot],
            device_id=device, device_id_type=MESH)

    def direct_part(source, slot, k, device):
        return pltpu.make_async_remote_copy(
            source.at[pl.ds(k * part, part)], slots.at[slot, pl.ds(k * part, part)],
            send.at[slot, k // per_chunk], recv.at[slot, k // per_chunk],
            device_id=device, device_id_type=MESH)

    def to_relay(source, side, k, device):
        return pltpu.make_async_remote_copy(
            source.at[pl.ds(k * part, part)], relay.at[side],
            send.at[FAR_T + side, k // per_chunk], relay_recv.at[side],
            device_id=device, device_id_type=MESH)

    def from_relay(side, device):
        return pltpu.make_async_remote_copy(
            relay.at[side], slots.at[FAR_T + side, pl.ds(pl.multiple_of(x * part, part), part)],
            relay_send.at[side], recv.at[FAR_T + side, x // per_chunk],
            device_id=device, device_id_type=MESH)

    for slot, source, ids in ((OWN_T, text, text_ids), (OWN_I, image, image_ids)):
        for k in range(chunks):
            local(source, slot, k).start()
        tags[slot] = ids[...]
    for side, ids in ((0, image_ids), (1, text_ids)):
        column_tags[side] = jnp.transpose(jnp.broadcast_to(ids[...], (rows, rows)))
    acc[...] = jnp.zeros_like(acc)
    loss_acc[...] = jnp.zeros_like(loss_acc)

    @pl.when(count > 0)
    def _():
        pl.semaphore_wait(barrier, count)

    reply(partner, answer.at[A_PARTNER])
    reply(ahead, answer.at[A_BEHIND])
    reply(behind, answer.at[A_AHEAD])
    reply(above, answer.at[A_BELOW])
    reply(below, answer.at[A_ABOVE])
    reply(source_t, answer_t.at[x], x > 0)
    reply(source_i, answer_i.at[x], x < last)
    for k in range(COLUMNS):
        if k > 0:
            reply(relay_t(k), answer.at[A_DEST_T], first)
        if k < last:
            reply(relay_i(k), answer.at[A_DEST_I], final)

    @pl.when(final)
    def _():
        for k in range(1, COLUMNS):
            hear(crossing(k), answer_t.at[k])
            to_relay(text, 0, k, crossing(k)).start()

    @pl.when(first)
    def _():
        for k in range(COLUMNS - 1):
            hear(crossing(k), answer_i.at[k])
            to_relay(image, 1, k, crossing(k)).start()

    def send_above():
        hear(above, answer.at[A_ABOVE])
        remote_tag(text_ids, CROSS_T, above).start()
        remote(text, CROSS_T, 0, above).start()

    def send_below():
        hear(below, answer.at[A_BELOW])
        remote_tag(image_ids, CROSS_I, below).start()
        remote(image, CROSS_I, 0, below).start()

    late_above = jnp.logical_and(b == 0, g == n_group - 1)
    top = z == depth - 1
    late_below = jnp.logical_or(jnp.logical_and(b == 0, g == 1), top)
    late_behind = jnp.logical_or(b < 2, jnp.logical_and(b == 2, g == 0))
    late_relay = jnp.logical_and(z == 0, low_y == 1)
    pl.when(jnp.logical_not(late_above))(send_above)
    pl.when(jnp.logical_not(late_below))(send_below)
    def send_ahead():
        hear(ahead, answer.at[A_AHEAD])
        remote_tag(text_ids, FAR_T, ahead).start()

        @pl.when(final)
        def _():
            direct_part(text, FAR_T, 0, ahead).start()

        @pl.when(jnp.logical_not(final))
        def _():
            remote(text, FAR_T, 0, ahead).start()

    def send_behind():
        hear(behind, answer.at[A_BEHIND])
        remote_tag(image_ids, FAR_I, behind).start()

        @pl.when(first)
        def _():
            direct_part(image, FAR_I, last, behind).start()

        @pl.when(jnp.logical_not(first))
        def _():
            remote(image, FAR_I, 0, behind).start()

    def send_rest():
        for k in range(1, chunks):
            remote(text, CROSS_T, k, above).start()
            remote(image, CROSS_I, k, below).start()

            @pl.when(jnp.logical_not(final))
            def _(k=k):
                remote(text, FAR_T, k, ahead).start()

            @pl.when(jnp.logical_not(first))
            def _(k=k):
                remote(image, FAR_I, k, behind).start()

    def pass_on(side):
        pltpu.make_async_copy(relay.at[side], relay.at[side], relay_recv.at[side]).wait()
        device = dest_t if side == 0 else dest_i
        hear(device, answer.at[A_DEST_T + side])
        from_relay(side, device).start()

    def score(side, slot, start, length):
        mine = slots[OWN_I if side == 0 else OWN_T]
        theirs = slots[slot, pl.ds(start, length)]
        scores = lax.dot_general(mine, theirs, (((1,), (1,)), ((), ())), preferred_element_type=jnp.float32)
        logits = logit_scale * scores + logit_bias
        matched = column_tags[side, :, :length] == tags[slot, :, pl.ds(start, length)]
        signed = jnp.where(matched, -logits, logits)
        small = jnp.exp(-jnp.abs(signed))
        sigmoid = jnp.where(signed >= 0, 1.0, small) / (1.0 + small)
        if side == 0:
            terms = jnp.maximum(signed, 0.0) + jnp.log1p(small)
            for k in range(length // CHUNK):
                loss_acc[...] += terms[:, k * CHUNK:(k + 1) * CHUNK]
        slopes = jnp.where(matched, -sigmoid, sigmoid).astype(jnp.bfloat16)
        acc[side] += jnp.dot(slopes, theirs, preferred_element_type=jnp.float32)

    send_ahead()
    pl.when(jnp.logical_not(late_behind))(send_behind)
    hear(partner, answer.at[A_PARTNER])

    @pl.when(core == 0)
    def _():
        remote_tag(text_ids, NEAR_T, partner).start()
        for k in range(chunks):
            remote(text, NEAR_T, k, partner).start()

    @pl.when(core == 1)
    def _():
        remote_tag(image_ids, NEAR_I, partner).start()
        for k in range(chunks):
            remote(image, NEAR_I, k, partner).start()

    for k in range(chunks):
        local(text, OWN_T, k).wait()
        local(image, OWN_I, k).wait()
    score(0, OWN_T, 0, rows)
    score(1, OWN_I, 0, rows)

    @pl.when(x > 0)
    def _():
        pass_on(0)

    pl.when(late_above)(send_above)
    pl.when(late_below)(send_below)

    @pl.when(jnp.logical_and(x < last, jnp.logical_not(late_relay)))
    def _():
        pass_on(1)

    late_rest = late_behind
    pl.when(jnp.logical_not(late_rest))(send_rest)

    @pl.when(late_rest)
    def _():
        for k in range(1, chunks):
            remote(text, CROSS_T, k, above).start()
            remote(image, CROSS_I, k, below).start()

            @pl.when(jnp.logical_not(final))
            def _(k=k):
                remote(text, FAR_T, k, ahead).start()

        send_behind()

        @pl.when(jnp.logical_not(first))
        def _():
            for k in range(1, chunks):
                remote(image, FAR_I, k, behind).start()

    def tags_far():
        remote_tag(text_ids, FAR_T, ahead).wait_recv()
        remote_tag(image_ids, FAR_I, behind).wait_recv()

        @pl.when(core == 0)
        def _():
            remote_tag(tags.at[FAR_I], NEAR_I, partner).start()

        @pl.when(core == 1)
        def _():
            remote_tag(tags.at[FAR_T], NEAR_T, partner).start()

    remote_tag(text_ids, CROSS_T, above).wait_recv()
    remote_tag(image_ids, CROSS_I, below).wait_recv()

    def far(k):
        for side, slot, source, device in ((0, FAR_T, text, ahead), (1, FAR_I, image, behind)):
            remote(source, slot, k, device).wait_recv()

            @pl.when(core == 1 - side)
            def _(side=side, slot=slot, k=k):
                remote(slots.at[slot], NEAR_T if side == 0 else NEAR_I, k, partner).start()

            score(side, slot, k * CHUNK, CHUNK)

    def cross(k):
        for side, slot, source, device in ((0, CROSS_T, text, above), (1, CROSS_I, image, below)):
            remote(source, slot, k, device).wait_recv()
            score(side, slot, k * CHUNK, CHUNK)

    def near():
        remote_tag(text_ids, NEAR_T, partner).wait_recv()
        remote_tag(image_ids, NEAR_I, partner).wait_recv()
        for side, slot, source in ((0, NEAR_T, text), (1, NEAR_I, image)):
            for k in range(chunks):
                remote(source, slot, k, partner).wait_recv()
            score(side, slot, 0, rows)

    @pl.when(b < 2)
    def _():
        cross(0)
        cross(1)
        tags_far()
        far(0)
        far(1)
        near()

    @pl.when(b >= 2)
    def _():
        tags_far()
        far(0)
        cross(0)
        far(1)

        @pl.when(jnp.logical_and(x < last, late_relay))
        def _():
            pass_on(1)

        near()
        cross(1)

    image_grad[...] = (logit_scale * acc[0]).astype(image_grad.dtype)
    text_grad[...] = (logit_scale * acc[1]).astype(text_grad.dtype)
    total = jnp.sum(jnp.transpose(loss_acc[...]), axis=0, keepdims=True)
    loss[...] = total / (4 * rows)

    for slot, source, ids, device in (
            (FAR_T, text, text_ids, ahead), (FAR_I, image, image_ids, behind),
            (CROSS_T, text, text_ids, above), (CROSS_I, image, image_ids, below),
            (NEAR_T, text, text_ids, partner), (NEAR_I, image, image_ids, partner)):
        remote_tag(ids, slot, device).wait_send()
        for k in range(chunks):
            remote(source, slot, k, device).wait_send()

    @pl.when(x > 0)
    def _():
        from_relay(0, dest_t).wait_send()

    @pl.when(x < last)
    def _():
        from_relay(1, dest_i).wait_send()


def write_out(loss, image_grad, text_grad, loss_out, image_out, text_out, done):
    piece = image_grad.shape[0] // PIECES
    copies = [pltpu.make_async_copy(loss, loss_out, done.at[2 * PIECES])]
    for i, (source, target) in enumerate(((image_grad, image_out), (text_grad, text_out))):
        for k in range(PIECES):
            part = pl.ds(k * piece, piece)
            copies.append(pltpu.make_async_copy(source.at[part], target.at[part], done.at[i * PIECES + k]))
    for copy in copies:
        copy.start()
    for copy in copies:
        copy.wait()


def per_device(n_group, n_blk, image_emb, text_emb, image_ids, text_ids):
    rows, width = image_emb.shape
    chunks = rows // CHUNK
    in_vmem = pl.BlockSpec(memory_space=pltpu.VMEM)
    in_hbm = pl.BlockSpec(memory_space=pltpu.HBM)
    shapes = ((1, rows), jnp.float32), ((rows, width), jnp.bfloat16), ((rows, width), jnp.bfloat16)
    results = pl.pallas_call(
        functools.partial(kernel, n_group, n_blk),
        out_shape=tuple(pltpu.VMEM(*s) for s in shapes),
        in_specs=[in_hbm, in_hbm, in_vmem, in_vmem],
        out_specs=(in_vmem, in_vmem, in_vmem),
        scratch_shapes=[
            pltpu.VMEM((8, rows, width), jnp.bfloat16),
            pltpu.VMEM((2, rows // COLUMNS, width), jnp.bfloat16),
            pltpu.VMEM((8, 1, rows), jnp.int32),
            pltpu.VMEM((2, rows, rows), jnp.int32),
            pltpu.VMEM((2, rows, width), jnp.float32),
            pltpu.VMEM((rows, CHUNK), jnp.float32),
            pltpu.SemaphoreType.DMA((8, chunks)),
            pltpu.SemaphoreType.DMA((8, chunks)),
            pltpu.SemaphoreType.DMA((8,)),
            pltpu.SemaphoreType.DMA((8,)),
            pltpu.SemaphoreType.DMA((2,)),
            pltpu.SemaphoreType.DMA((2,)),
            pltpu.SemaphoreType.REGULAR((7,)),
            pltpu.SemaphoreType.REGULAR((COLUMNS,)),
            pltpu.SemaphoreType.REGULAR((COLUMNS,)),
        ],
        compiler_params=pltpu.CompilerParams(collective_id=0, has_side_effects=True, vmem_limit_bytes=56 * 2**20),
        cost_estimate=pl.CostEstimate(flops=2 * 16 * rows * rows * width, bytes_accessed=8 * rows * width, transcendentals=0),
    )(image_emb, text_emb, image_ids.reshape(1, rows), text_ids.reshape(1, rows))
    loss, image_grad, text_grad = pl.pallas_call(
        write_out,
        out_shape=tuple(jax.ShapeDtypeStruct(*s) for s in shapes),
        in_specs=[in_vmem] * 3,
        out_specs=(in_hbm, in_hbm, in_hbm),
        scratch_shapes=[pltpu.SemaphoreType.DMA((2 * PIECES + 1,))],
        compiler_params=pltpu.CompilerParams(vmem_limit_bytes=4 * 2**20),
    )(*results)
    return loss.reshape(rows), image_grad, text_grad


def solution(mesh):
    sizes = dict(mesh.shape)
    vector, matrix = P(("group", "blk")), P(("group", "blk"), None)
    return jax.shard_map(
        functools.partial(per_device, sizes["group"], sizes["blk"]), mesh=mesh,
        in_specs=(matrix, matrix, vector, vector), out_specs=(vector, matrix, matrix), check_vma=False)
```

```python
import functools

import jax
import jax.numpy as jnp
from jax import lax
from jax.experimental import pallas as pl
from jax.experimental.pallas import tpu as pltpu
from jax.sharding import PartitionSpec as P

logit_scale = 10.0
logit_bias = -3.0
MESH = pl.DeviceIdType.MESH
CHUNK = 128
COLUMNS = 8
EARLY = 192
PIECES = 4

OWN_T, OWN_I, FAR_T, FAR_I, NEAR_T, NEAR_I, CROSS_T, CROSS_I = range(8)
A_PARTNER, A_AHEAD, A_BEHIND, A_ABOVE, A_BELOW, A_DEST_T, A_DEST_I = range(7)


def kernel(n_group, n_blk, image, text, image_ids, text_ids, loss, image_grad, text_grad,
           slots, relay, tags, column_tags, acc, loss_acc,
           send, recv, tag_send, tag_recv, relay_send, relay_recv, answer, answer_t, answer_i):
    g, b = lax.axis_index("group"), lax.axis_index("blk")
    rows = image.shape[0]
    chunks = rows // CHUNK
    part = rows // COLUMNS
    per_chunk = CHUNK // part
    depth = n_blk // (4 * COLUMNS)
    core, x = lax.rem(b, 2), lax.rem(b // 2, COLUMNS)
    low_y, z = lax.rem(b // (2 * COLUMNS), 2), b // (4 * COLUMNS)
    last = COLUMNS - 1

    def at(z_, y_, x_):
        return (g, z_ * (4 * COLUMNS) + y_ * (2 * COLUMNS) + x_ * 2 + core)

    partner = (g, b + 1 - 2 * core)
    ahead, behind = (g, lax.rem(b + 2, n_blk)), (g, lax.rem(b + n_blk - 2, n_blk))
    above, below = (lax.rem(g + 1, n_group), b), (lax.rem(g + n_group - 1, n_group), b)

    def crossing(k):
        return at(z, 1 - low_y, k)

    source_t, source_i = at(z, 1 - low_y, last), at(z, 1 - low_y, 0)
    dest_t = at(lax.rem(z + 1 - low_y, depth), low_y, 0)
    dest_i = at(lax.rem(z + depth - low_y, depth), low_y, last)

    def relay_t(k):
        return at(lax.rem(z + depth - 1 + low_y, depth), low_y, k)

    def relay_i(k):
        return at(lax.rem(z + low_y, depth), low_y, k)

    def order(device):
        index = device[0] * n_blk + device[1]
        return jnp.where(index == 0, n_group * n_blk, index)

    me = order((g, b))

    def lower(device):
        return order(device) < me

    first, final = x == 0, x == last
    barrier = pltpu.get_barrier_semaphore()

    def announce(device, when=True):
        @pl.when(jnp.logical_and(when, me < order(device)))
        def _():
            pl.semaphore_signal(barrier, inc=1, device_id=device, device_id_type=MESH)

    def reply(device, semaphore, when=True):
        @pl.when(jnp.logical_and(when, lower(device)))
        def _():
            pl.semaphore_signal(semaphore, inc=1, device_id=device, device_id_type=MESH)

    def hear(device, semaphore, when=True):
        @pl.when(jnp.logical_and(when, me < order(device)))
        def _():
            pl.semaphore_wait(semaphore, 1)

    count = jnp.int32(0)
    for device, when in ((partner, True), (ahead, True), (behind, True), (above, True), (below, True),
                         (source_t, x > 0), (source_i, x < last), (dest_t, x > 0), (dest_i, x < last)):
        announce(device, when)
        count += jnp.where(jnp.logical_and(when, lower(device)), 1, 0)
    for k in range(COLUMNS):
        for device, when in ((crossing(k), final if k > 0 else None), (crossing(k), first if k < last else None),
                             (relay_t(k), first if k > 0 else None), (relay_i(k), final if k < last else None)):
            if when is not None:
                announce(device, when)
                count += jnp.where(jnp.logical_and(when, lower(device)), 1, 0)

    def span(k):
        return pl.ds(k * CHUNK, CHUNK)

    def local(source, slot, k):
        return pltpu.make_async_copy(source.at[span(k)], slots.at[slot, span(k)], recv.at[slot, k])

    def remote(source, slot, k, device):
        return pltpu.make_async_remote_copy(
            source.at[span(k)], slots.at[slot, span(k)], send.at[slot, k], recv.at[slot, k],
            device_id=device, device_id_type=MESH)

    def bulk(source, slot, device, early):
        spans = []
        for k in range(chunks):
            low, high = max(k * CHUNK, 0 if early else EARLY), min((k + 1) * CHUNK, EARLY if early else rows)
            if low < high:
                spans.append((k, pl.ds(low, high - low)))
        return [pltpu.make_async_remote_copy(
            source.at[part_], slots.at[slot, part_], send.at[slot, k], recv.at[slot, k],
            device_id=device, device_id_type=MESH) for k, part_ in spans]

    def start(copies):
        for copy in copies:
            copy.start()

    def remote_tag(source, slot, device):
        return pltpu.make_async_remote_copy(
            source, tags.at[slot], tag_send.at[slot], tag_recv.at[slot],
            device_id=device, device_id_type=MESH)

    def direct_part(source, slot, k, device):
        return pltpu.make_async_remote_copy(
            source.at[pl.ds(k * part, part)], slots.at[slot, pl.ds(k * part, part)],
            send.at[slot, k // per_chunk], recv.at[slot, k // per_chunk],
            device_id=device, device_id_type=MESH)

    def to_relay(source, side, k, device):
        return pltpu.make_async_remote_copy(
            source.at[pl.ds(k * part, part)], relay.at[side],
            send.at[FAR_T + side, k // per_chunk], relay_recv.at[side],
            device_id=device, device_id_type=MESH)

    def from_relay(side, device):
        return pltpu.make_async_remote_copy(
            relay.at[side], slots.at[FAR_T + side, pl.ds(pl.multiple_of(x * part, part), part)],
            relay_send.at[side], recv.at[FAR_T + side, x // per_chunk],
            device_id=device, device_id_type=MESH)

    for slot, source, ids in ((OWN_T, text, text_ids), (OWN_I, image, image_ids)):
        for k in range(chunks):
            local(source, slot, k).start()
        tags[slot] = ids[...]
    for side, ids in ((0, image_ids), (1, text_ids)):
        column_tags[side] = jnp.transpose(jnp.broadcast_to(ids[...], (rows, rows)))
    acc[...] = jnp.zeros_like(acc)
    loss_acc[...] = jnp.zeros_like(loss_acc)

    @pl.when(count > 0)
    def _():
        pl.semaphore_wait(barrier, count)

    reply(partner, answer.at[A_PARTNER])
    reply(ahead, answer.at[A_BEHIND])
    reply(behind, answer.at[A_AHEAD])
    reply(above, answer.at[A_BELOW])
    reply(below, answer.at[A_ABOVE])
    reply(source_t, answer_t.at[x], x > 0)
    reply(source_i, answer_i.at[x], x < last)
    for k in range(COLUMNS):
        if k > 0:
            reply(relay_t(k), answer.at[A_DEST_T], first)
        if k < last:
            reply(relay_i(k), answer.at[A_DEST_I], final)

    @pl.when(final)
    def _():
        for k in range(1, COLUMNS):
            hear(crossing(k), answer_t.at[k])
            to_relay(text, 0, k, crossing(k)).start()

    @pl.when(first)
    def _():
        for k in range(COLUMNS - 1):
            hear(crossing(k), answer_i.at[k])
            to_relay(image, 1, k, crossing(k)).start()

    def send_above():
        hear(above, answer.at[A_ABOVE])
        remote_tag(text_ids, CROSS_T, above).start()
        start(bulk(text, CROSS_T, above, True))

    def send_below():
        hear(below, answer.at[A_BELOW])
        remote_tag(image_ids, CROSS_I, below).start()
        start(bulk(image, CROSS_I, below, True))

    late_above = jnp.logical_and(b == 0, g == n_group - 1)
    top = z == depth - 1
    late_below = jnp.logical_or(jnp.logical_and(b == 0, g == 1), top)
    late_behind = jnp.logical_or(b < 2, jnp.logical_and(b == 2, g == 0))
    late_relay = jnp.logical_and(z == 0, low_y == 1)
    pl.when(jnp.logical_not(late_above))(send_above)
    pl.when(jnp.logical_not(late_below))(send_below)
    def send_ahead():
        hear(ahead, answer.at[A_AHEAD])
        remote_tag(text_ids, FAR_T, ahead).start()

        @pl.when(final)
        def _():
            direct_part(text, FAR_T, 0, ahead).start()

        @pl.when(jnp.logical_not(final))
        def _():
            start(bulk(text, FAR_T, ahead, True))

    def send_behind():
        hear(behind, answer.at[A_BEHIND])
        remote_tag(image_ids, FAR_I, behind).start()

        @pl.when(first)
        def _():
            direct_part(image, FAR_I, last, behind).start()

        @pl.when(jnp.logical_not(first))
        def _():
            start(bulk(image, FAR_I, behind, True))

    def send_rest(with_behind=True):
        start(bulk(text, CROSS_T, above, False))
        start(bulk(image, CROSS_I, below, False))
        pl.when(jnp.logical_not(final))(lambda: start(bulk(text, FAR_T, ahead, False)))
        if with_behind:
            pl.when(jnp.logical_not(first))(lambda: start(bulk(image, FAR_I, behind, False)))

    def pass_on(side):
        pltpu.make_async_copy(relay.at[side], relay.at[side], relay_recv.at[side]).wait()
        device = dest_t if side == 0 else dest_i
        hear(device, answer.at[A_DEST_T + side])
        from_relay(side, device).start()

    def score(side, slot, start, length):
        mine = slots[OWN_I if side == 0 else OWN_T]
        theirs = slots[slot, pl.ds(start, length)]
        scores = lax.dot_general(mine, theirs, (((1,), (1,)), ((), ())), preferred_element_type=jnp.float32)
        logits = logit_scale * scores + logit_bias
        matched = column_tags[side, :, :length] == tags[slot, :, pl.ds(start, length)]
        signed = jnp.where(matched, -logits, logits)
        small = jnp.exp(-jnp.abs(signed))
        sigmoid = jnp.where(signed >= 0, 1.0, small) / (1.0 + small)
        if side == 0:
            terms = jnp.maximum(signed, 0.0) + jnp.log1p(small)
            for k in range(length // CHUNK):
                loss_acc[...] += terms[:, k * CHUNK:(k + 1) * CHUNK]
        slopes = jnp.where(matched, -sigmoid, sigmoid).astype(jnp.bfloat16)
        acc[side] += jnp.dot(slopes, theirs, preferred_element_type=jnp.float32)

    send_ahead()
    pl.when(jnp.logical_not(late_behind))(send_behind)
    hear(partner, answer.at[A_PARTNER])

    @pl.when(core == 0)
    def _():
        remote_tag(text_ids, NEAR_T, partner).start()
        for k in range(chunks):
            remote(text, NEAR_T, k, partner).start()

    @pl.when(core == 1)
    def _():
        remote_tag(image_ids, NEAR_I, partner).start()
        for k in range(chunks):
            remote(image, NEAR_I, k, partner).start()

    for k in range(chunks):
        local(text, OWN_T, k).wait()
        local(image, OWN_I, k).wait()
    score(0, OWN_T, 0, rows)
    score(1, OWN_I, 0, rows)

    pl.when(jnp.logical_and(top, low_y == 1))(send_below)

    @pl.when(x > 0)
    def _():
        pass_on(0)

    pl.when(late_above)(send_above)
    pl.when(jnp.logical_and(late_below, jnp.logical_not(jnp.logical_and(top, low_y == 1))))(send_below)

    @pl.when(jnp.logical_and(x < last, jnp.logical_not(late_relay)))
    def _():
        pass_on(1)

    pl.when(jnp.logical_not(late_behind))(send_rest)

    @pl.when(late_behind)
    def _():
        send_rest(False)
        send_behind()
        pl.when(jnp.logical_not(first))(lambda: start(bulk(image, FAR_I, behind, False)))

    def far(side, k):
        slot, source, ids, device = ((FAR_T, text, text_ids, ahead), (FAR_I, image, image_ids, behind))[side]
        twin = (NEAR_T, NEAR_I)[side]
        if k == 0:
            remote_tag(ids, slot, device).wait_recv()
            pl.when(core == 1 - side)(lambda: remote_tag(tags.at[slot], twin, partner).start())
        remote(source, slot, k, device).wait_recv()
        pl.when(core == 1 - side)(lambda: remote(slots.at[slot], twin, k, partner).start())
        score(side, slot, k * CHUNK, CHUNK)

    def cross(side, k):
        slot, source, ids, device = ((CROSS_T, text, text_ids, above), (CROSS_I, image, image_ids, below))[side]
        if k == 0:
            remote_tag(ids, slot, device).wait_recv()
        remote(source, slot, k, device).wait_recv()
        score(side, slot, k * CHUNK, CHUNK)

    def near(side):
        slot, source, ids = ((NEAR_T, text, text_ids), (NEAR_I, image, image_ids))[side]
        remote_tag(ids, slot, partner).wait_recv()
        for k in range(chunks):
            remote(source, slot, k, partner).wait_recv()
        score(side, slot, 0, rows)

    @pl.when(b < 2)
    def _():
        far(1, 0)
        far(1, 1)
        near(1)
        cross(0, 0)
        cross(1, 0)
        cross(0, 1)
        cross(1, 1)
        pl.when(core == 1)(lambda: near(0))
        far(0, 0)
        far(0, 1)
        pl.when(core == 0)(lambda: near(0))

    @pl.when(b >= 2)
    def _():
        far(0, 0)
        far(1, 0)
        cross(0, 0)
        cross(1, 0)
        far(0, 1)
        far(1, 1)

        @pl.when(jnp.logical_and(x < last, late_relay))
        def _():
            pass_on(1)

        near(0)
        near(1)
        cross(0, 1)
        cross(1, 1)

    image_grad[...] = (logit_scale * acc[0]).astype(image_grad.dtype)
    text_grad[...] = (logit_scale * acc[1]).astype(text_grad.dtype)
    total = jnp.sum(jnp.transpose(loss_acc[...]), axis=0, keepdims=True)
    loss[...] = total / (4 * rows)

    for slot, source, ids, device in (
            (FAR_T, text, text_ids, ahead), (FAR_I, image, image_ids, behind),
            (CROSS_T, text, text_ids, above), (CROSS_I, image, image_ids, below),
            (NEAR_T, text, text_ids, partner), (NEAR_I, image, image_ids, partner)):
        remote_tag(ids, slot, device).wait_send()
        for k in range(chunks):
            remote(source, slot, k, device).wait_send()

    @pl.when(x > 0)
    def _():
        from_relay(0, dest_t).wait_send()

    @pl.when(x < last)
    def _():
        from_relay(1, dest_i).wait_send()


def write_out(loss, image_grad, text_grad, loss_out, image_out, text_out, done):
    piece = image_grad.shape[0] // PIECES
    copies = [pltpu.make_async_copy(loss, loss_out, done.at[2 * PIECES])]
    for i, (source, target) in enumerate(((image_grad, image_out), (text_grad, text_out))):
        for k in range(PIECES):
            part = pl.ds(k * piece, piece)
            copies.append(pltpu.make_async_copy(source.at[part], target.at[part], done.at[i * PIECES + k]))
    for copy in copies:
        copy.start()
    for copy in copies:
        copy.wait()


def per_device(n_group, n_blk, image_emb, text_emb, image_ids, text_ids):
    rows, width = image_emb.shape
    chunks = rows // CHUNK
    in_vmem = pl.BlockSpec(memory_space=pltpu.VMEM)
    in_hbm = pl.BlockSpec(memory_space=pltpu.HBM)
    shapes = ((1, rows), jnp.float32), ((rows, width), jnp.bfloat16), ((rows, width), jnp.bfloat16)
    results = pl.pallas_call(
        functools.partial(kernel, n_group, n_blk),
        out_shape=tuple(pltpu.VMEM(*s) for s in shapes),
        in_specs=[in_hbm, in_hbm, in_vmem, in_vmem],
        out_specs=(in_vmem, in_vmem, in_vmem),
        scratch_shapes=[
            pltpu.VMEM((8, rows, width), jnp.bfloat16),
            pltpu.VMEM((2, rows // COLUMNS, width), jnp.bfloat16),
            pltpu.VMEM((8, 1, rows), jnp.int32),
            pltpu.VMEM((2, rows, rows), jnp.int32),
            pltpu.VMEM((2, rows, width), jnp.float32),
            pltpu.VMEM((rows, CHUNK), jnp.float32),
            pltpu.SemaphoreType.DMA((8, chunks)),
            pltpu.SemaphoreType.DMA((8, chunks)),
            pltpu.SemaphoreType.DMA((8,)),
            pltpu.SemaphoreType.DMA((8,)),
            pltpu.SemaphoreType.DMA((2,)),
            pltpu.SemaphoreType.DMA((2,)),
            pltpu.SemaphoreType.REGULAR((7,)),
            pltpu.SemaphoreType.REGULAR((COLUMNS,)),
            pltpu.SemaphoreType.REGULAR((COLUMNS,)),
        ],
        compiler_params=pltpu.CompilerParams(collective_id=0, has_side_effects=True, vmem_limit_bytes=56 * 2**20),
        cost_estimate=pl.CostEstimate(flops=2 * 16 * rows * rows * width, bytes_accessed=8 * rows * width, transcendentals=0),
    )(image_emb, text_emb, image_ids.reshape(1, rows), text_ids.reshape(1, rows))
    loss, image_grad, text_grad = pl.pallas_call(
        write_out,
        out_shape=tuple(jax.ShapeDtypeStruct(*s) for s in shapes),
        in_specs=[in_vmem] * 3,
        out_specs=(in_hbm, in_hbm, in_hbm),
        scratch_shapes=[pltpu.SemaphoreType.DMA((2 * PIECES + 1,))],
        compiler_params=pltpu.CompilerParams(vmem_limit_bytes=4 * 2**20),
    )(*results)
    return loss.reshape(rows), image_grad, text_grad


def solution(mesh):
    sizes = dict(mesh.shape)
    vector, matrix = P(("group", "blk")), P(("group", "blk"), None)
    return jax.shard_map(
        functools.partial(per_device, sizes["group"], sizes["blk"]), mesh=mesh,
        in_specs=(matrix, matrix, vector, vector), out_specs=(vector, matrix, matrix), check_vma=False)
```

```python
import functools

import jax
import jax.numpy as jnp
from jax import lax
from jax.experimental import pallas as pl
from jax.experimental.pallas import tpu as pltpu
from jax.sharding import PartitionSpec as P

logit_scale = 10.0
logit_bias = -3.0
MESH = pl.DeviceIdType.MESH
CHUNK = 128
COLUMNS = 8
EARLY = 192
PIECES = 4

OWN_T, OWN_I, FAR_T, FAR_I, NEAR_T, NEAR_I, CROSS_T, CROSS_I = range(8)
A_PARTNER, A_AHEAD, A_BEHIND, A_ABOVE, A_BELOW, A_DEST_T, A_DEST_I = range(7)


def kernel(n_group, n_blk, image, text, image_ids, text_ids, loss, image_grad, text_grad,
           slots, relay, tags, column_tags, acc, loss_acc,
           send, recv, tag_send, tag_recv, relay_send, relay_recv, answer, answer_t, answer_i):
    g, b = lax.axis_index("group"), lax.axis_index("blk")
    rows = image.shape[0]
    chunks = rows // CHUNK
    part = rows // COLUMNS
    per_chunk = CHUNK // part
    depth = n_blk // (4 * COLUMNS)
    core, x = lax.rem(b, 2), lax.rem(b // 2, COLUMNS)
    low_y, z = lax.rem(b // (2 * COLUMNS), 2), b // (4 * COLUMNS)
    last = COLUMNS - 1

    def at(z_, y_, x_):
        return (g, z_ * (4 * COLUMNS) + y_ * (2 * COLUMNS) + x_ * 2 + core)

    partner = (g, b + 1 - 2 * core)
    ahead, behind = (g, lax.rem(b + 2, n_blk)), (g, lax.rem(b + n_blk - 2, n_blk))
    above, below = (lax.rem(g + 1, n_group), b), (lax.rem(g + n_group - 1, n_group), b)

    def crossing(k):
        return at(z, 1 - low_y, k)

    source_t, source_i = at(z, 1 - low_y, last), at(z, 1 - low_y, 0)
    dest_t = at(lax.rem(z + 1 - low_y, depth), low_y, 0)
    dest_i = at(lax.rem(z + depth - low_y, depth), low_y, last)

    def relay_t(k):
        return at(lax.rem(z + depth - 1 + low_y, depth), low_y, k)

    def relay_i(k):
        return at(lax.rem(z + low_y, depth), low_y, k)

    def order(device):
        index = device[0] * n_blk + device[1]
        return jnp.where(index == 0, n_group * n_blk, index)

    me = order((g, b))

    def lower(device):
        return order(device) < me

    first, final = x == 0, x == last
    barrier = pltpu.get_barrier_semaphore()

    def announce(device, when=True):
        @pl.when(jnp.logical_and(when, me < order(device)))
        def _():
            pl.semaphore_signal(barrier, inc=1, device_id=device, device_id_type=MESH)

    def reply(device, semaphore, when=True):
        @pl.when(jnp.logical_and(when, lower(device)))
        def _():
            pl.semaphore_signal(semaphore, inc=1, device_id=device, device_id_type=MESH)

    def hear(device, semaphore, when=True):
        @pl.when(jnp.logical_and(when, me < order(device)))
        def _():
            pl.semaphore_wait(semaphore, 1)

    count = jnp.int32(0)
    for device, when in ((partner, True), (ahead, True), (behind, True), (above, True), (below, True),
                         (source_t, x > 0), (source_i, x < last), (dest_t, x > 0), (dest_i, x < last)):
        announce(device, when)
        count += jnp.where(jnp.logical_and(when, lower(device)), 1, 0)
    for k in range(COLUMNS):
        for device, when in ((crossing(k), final if k > 0 else None), (crossing(k), first if k < last else None),
                             (relay_t(k), first if k > 0 else None), (relay_i(k), final if k < last else None)):
            if when is not None:
                announce(device, when)
                count += jnp.where(jnp.logical_and(when, lower(device)), 1, 0)

    def span(k):
        return pl.ds(k * CHUNK, CHUNK)

    def local(source, slot, k):
        return pltpu.make_async_copy(source.at[span(k)], slots.at[slot, span(k)], recv.at[slot, k])

    def remote(source, slot, k, device):
        return pltpu.make_async_remote_copy(
            source.at[span(k)], slots.at[slot, span(k)], send.at[slot, k], recv.at[slot, k],
            device_id=device, device_id_type=MESH)

    def bulk(source, slot, device, early):
        spans = []
        for k in range(chunks):
            low, high = max(k * CHUNK, 0 if early else EARLY), min((k + 1) * CHUNK, EARLY if early else rows)
            if low < high:
                spans.append((k, pl.ds(low, high - low)))
        return [pltpu.make_async_remote_copy(
            source.at[part_], slots.at[slot, part_], send.at[slot, k], recv.at[slot, k],
            device_id=device, device_id_type=MESH) for k, part_ in spans]

    def start(copies):
        for copy in copies:
            copy.start()

    def remote_tag(source, slot, device):
        return pltpu.make_async_remote_copy(
            source, tags.at[slot], tag_send.at[slot], tag_recv.at[slot],
            device_id=device, device_id_type=MESH)

    def direct_part(source, slot, k, device):
        return pltpu.make_async_remote_copy(
            source.at[pl.ds(k * part, part)], slots.at[slot, pl.ds(k * part, part)],
            send.at[slot, k // per_chunk], recv.at[slot, k // per_chunk],
            device_id=device, device_id_type=MESH)

    def to_relay(source, side, k, device):
        return pltpu.make_async_remote_copy(
            source.at[pl.ds(k * part, part)], relay.at[side],
            send.at[FAR_T + side, k // per_chunk], relay_recv.at[side],
            device_id=device, device_id_type=MESH)

    def from_relay(side, device):
        return pltpu.make_async_remote_copy(
            relay.at[side], slots.at[FAR_T + side, pl.ds(pl.multiple_of(x * part, part), part)],
            relay_send.at[side], recv.at[FAR_T + side, x // per_chunk],
            device_id=device, device_id_type=MESH)

    for slot, source, ids in ((OWN_T, text, text_ids), (OWN_I, image, image_ids)):
        for k in range(chunks):
            local(source, slot, k).start()
        tags[slot] = ids[...]

    @pl.when(count > 0)
    def _():
        pl.semaphore_wait(barrier, count)

    reply(partner, answer.at[A_PARTNER])
    reply(ahead, answer.at[A_BEHIND])
    reply(behind, answer.at[A_AHEAD])
    reply(above, answer.at[A_BELOW])
    reply(below, answer.at[A_ABOVE])
    reply(source_t, answer_t.at[x], x > 0)
    reply(source_i, answer_i.at[x], x < last)
    for k in range(COLUMNS):
        if k > 0:
            reply(relay_t(k), answer.at[A_DEST_T], first)
        if k < last:
            reply(relay_i(k), answer.at[A_DEST_I], final)

    @pl.when(final)
    def _():
        for k in range(1, COLUMNS):
            hear(crossing(k), answer_t.at[k])
            to_relay(text, 0, k, crossing(k)).start()

    @pl.when(first)
    def _():
        for k in range(COLUMNS - 1):
            hear(crossing(k), answer_i.at[k])
            to_relay(image, 1, k, crossing(k)).start()

    def send_above():
        hear(above, answer.at[A_ABOVE])
        remote_tag(text_ids, CROSS_T, above).start()
        start(bulk(text, CROSS_T, above, True))

    def send_below():
        hear(below, answer.at[A_BELOW])
        remote_tag(image_ids, CROSS_I, below).start()
        start(bulk(image, CROSS_I, below, True))

    late_above = jnp.logical_and(b == 0, g == n_group - 1)
    top = z == depth - 1
    late_below = jnp.logical_or(jnp.logical_and(b == 0, g == 1), top)
    late_behind = jnp.logical_or(b < 2, jnp.logical_and(b == 2, g == 0))
    late_relay = jnp.logical_and(z == 0, low_y == 1)
    pl.when(jnp.logical_not(late_above))(send_above)
    pl.when(jnp.logical_not(late_below))(send_below)
    def send_ahead():
        hear(ahead, answer.at[A_AHEAD])
        remote_tag(text_ids, FAR_T, ahead).start()

        @pl.when(final)
        def _():
            direct_part(text, FAR_T, 0, ahead).start()

        @pl.when(jnp.logical_not(final))
        def _():
            start(bulk(text, FAR_T, ahead, True))

    def send_behind():
        hear(behind, answer.at[A_BEHIND])
        remote_tag(image_ids, FAR_I, behind).start()

        @pl.when(first)
        def _():
            direct_part(image, FAR_I, last, behind).start()

        @pl.when(jnp.logical_not(first))
        def _():
            start(bulk(image, FAR_I, behind, True))

    def send_rest(with_behind=True):
        start(bulk(text, CROSS_T, above, False))
        start(bulk(image, CROSS_I, below, False))
        pl.when(jnp.logical_not(final))(lambda: start(bulk(text, FAR_T, ahead, False)))
        if with_behind:
            pl.when(jnp.logical_not(first))(lambda: start(bulk(image, FAR_I, behind, False)))

    def pass_on(side):
        pltpu.make_async_copy(relay.at[side], relay.at[side], relay_recv.at[side]).wait()
        device = dest_t if side == 0 else dest_i
        hear(device, answer.at[A_DEST_T + side])
        from_relay(side, device).start()

    def score(side, slot, start, length):
        mine = slots[OWN_I if side == 0 else OWN_T]
        theirs = slots[slot, pl.ds(start, length)]
        scores = lax.dot_general(mine, theirs, (((1,), (1,)), ((), ())), preferred_element_type=jnp.float32)
        logits = logit_scale * scores + logit_bias
        matched = column_tags[side, :, :length] == tags[slot, :, pl.ds(start, length)]
        signed = jnp.where(matched, -logits, logits)
        small = jnp.exp(-jnp.abs(signed))
        sigmoid = jnp.where(signed >= 0, 1.0, small) / (1.0 + small)
        if side == 0:
            terms = jnp.maximum(signed, 0.0) + jnp.log1p(small)
            for k in range(length // CHUNK):
                loss_acc[...] += terms[:, k * CHUNK:(k + 1) * CHUNK]
        slopes = jnp.where(matched, -sigmoid, sigmoid).astype(jnp.bfloat16)
        acc[side] += jnp.dot(slopes, theirs, preferred_element_type=jnp.float32)

    send_ahead()
    pl.when(jnp.logical_not(late_behind))(send_behind)
    hear(partner, answer.at[A_PARTNER])

    @pl.when(core == 0)
    def _():
        remote_tag(text_ids, NEAR_T, partner).start()
        for k in range(chunks):
            remote(text, NEAR_T, k, partner).start()

    @pl.when(core == 1)
    def _():
        remote_tag(image_ids, NEAR_I, partner).start()
        for k in range(chunks):
            remote(image, NEAR_I, k, partner).start()

    for side, ids in ((0, image_ids), (1, text_ids)):
        column_tags[side] = jnp.transpose(jnp.broadcast_to(ids[...], (rows, rows)))
    acc[...] = jnp.zeros_like(acc)
    loss_acc[...] = jnp.zeros_like(loss_acc)
    for k in range(chunks):
        local(text, OWN_T, k).wait()
        local(image, OWN_I, k).wait()
    score(0, OWN_T, 0, rows)
    score(1, OWN_I, 0, rows)

    pl.when(jnp.logical_and(top, low_y == 1))(send_below)

    @pl.when(x > 0)
    def _():
        pass_on(0)

    pl.when(late_above)(send_above)
    pl.when(jnp.logical_and(late_below, jnp.logical_not(jnp.logical_and(top, low_y == 1))))(send_below)

    @pl.when(jnp.logical_and(x < last, jnp.logical_not(late_relay)))
    def _():
        pass_on(1)

    pl.when(jnp.logical_not(late_behind))(send_rest)

    @pl.when(late_behind)
    def _():
        send_rest(False)
        send_behind()
        pl.when(jnp.logical_not(first))(lambda: start(bulk(image, FAR_I, behind, False)))

    def far(side, k):
        slot, source, ids, device = ((FAR_T, text, text_ids, ahead), (FAR_I, image, image_ids, behind))[side]
        twin = (NEAR_T, NEAR_I)[side]
        if k == 0:
            remote_tag(ids, slot, device).wait_recv()
            pl.when(core == 1 - side)(lambda: remote_tag(tags.at[slot], twin, partner).start())
        remote(source, slot, k, device).wait_recv()
        pl.when(core == 1 - side)(lambda: remote(slots.at[slot], twin, k, partner).start())
        score(side, slot, k * CHUNK, CHUNK)

    def cross(side, k):
        slot, source, ids, device = ((CROSS_T, text, text_ids, above), (CROSS_I, image, image_ids, below))[side]
        if k == 0:
            remote_tag(ids, slot, device).wait_recv()
        remote(source, slot, k, device).wait_recv()
        score(side, slot, k * CHUNK, CHUNK)

    def near(side):
        slot, source, ids = ((NEAR_T, text, text_ids), (NEAR_I, image, image_ids))[side]
        remote_tag(ids, slot, partner).wait_recv()
        for k in range(chunks):
            remote(source, slot, k, partner).wait_recv()
        score(side, slot, 0, rows)

    @pl.when(b < 2)
    def _():
        far(1, 0)
        far(1, 1)
        near(1)
        cross(0, 0)
        cross(1, 0)
        cross(0, 1)
        cross(1, 1)
        pl.when(core == 1)(lambda: near(0))
        far(0, 0)
        far(0, 1)
        pl.when(core == 0)(lambda: near(0))

    @pl.when(b >= 2)
    def _():
        far(0, 0)
        far(1, 0)
        cross(0, 0)
        cross(1, 0)
        far(0, 1)
        far(1, 1)

        @pl.when(jnp.logical_and(x < last, late_relay))
        def _():
            pass_on(1)

        near(0)
        near(1)
        cross(0, 1)
        cross(1, 1)

    image_grad[...] = (logit_scale * acc[0]).astype(image_grad.dtype)
    text_grad[...] = (logit_scale * acc[1]).astype(text_grad.dtype)
    total = jnp.sum(jnp.transpose(loss_acc[...]), axis=0, keepdims=True)
    loss[...] = total / (4 * rows)

    for slot, source, ids, device in (
            (FAR_T, text, text_ids, ahead), (FAR_I, image, image_ids, behind),
            (CROSS_T, text, text_ids, above), (CROSS_I, image, image_ids, below),
            (NEAR_T, text, text_ids, partner), (NEAR_I, image, image_ids, partner)):
        remote_tag(ids, slot, device).wait_send()
        for k in range(chunks):
            remote(source, slot, k, device).wait_send()

    @pl.when(x > 0)
    def _():
        from_relay(0, dest_t).wait_send()

    @pl.when(x < last)
    def _():
        from_relay(1, dest_i).wait_send()


def write_out(loss, image_grad, text_grad, loss_out, image_out, text_out, done):
    piece = image_grad.shape[0] // PIECES
    copies = [pltpu.make_async_copy(loss, loss_out, done.at[2 * PIECES])]
    for i, (source, target) in enumerate(((image_grad, image_out), (text_grad, text_out))):
        for k in range(PIECES):
            part = pl.ds(k * piece, piece)
            copies.append(pltpu.make_async_copy(source.at[part], target.at[part], done.at[i * PIECES + k]))
    for copy in copies:
        copy.start()
    for copy in copies:
        copy.wait()


def per_device(n_group, n_blk, image_emb, text_emb, image_ids, text_ids):
    rows, width = image_emb.shape
    chunks = rows // CHUNK
    in_vmem = pl.BlockSpec(memory_space=pltpu.VMEM)
    in_hbm = pl.BlockSpec(memory_space=pltpu.HBM)
    shapes = ((1, rows), jnp.float32), ((rows, width), jnp.bfloat16), ((rows, width), jnp.bfloat16)
    results = pl.pallas_call(
        functools.partial(kernel, n_group, n_blk),
        out_shape=tuple(pltpu.VMEM(*s) for s in shapes),
        in_specs=[in_hbm, in_hbm, in_vmem, in_vmem],
        out_specs=(in_vmem, in_vmem, in_vmem),
        scratch_shapes=[
            pltpu.VMEM((8, rows, width), jnp.bfloat16),
            pltpu.VMEM((2, rows // COLUMNS, width), jnp.bfloat16),
            pltpu.VMEM((8, 1, rows), jnp.int32),
            pltpu.VMEM((2, rows, rows), jnp.int32),
            pltpu.VMEM((2, rows, width), jnp.float32),
            pltpu.VMEM((rows, CHUNK), jnp.float32),
            pltpu.SemaphoreType.DMA((8, chunks)),
            pltpu.SemaphoreType.DMA((8, chunks)),
            pltpu.SemaphoreType.DMA((8,)),
            pltpu.SemaphoreType.DMA((8,)),
            pltpu.SemaphoreType.DMA((2,)),
            pltpu.SemaphoreType.DMA((2,)),
            pltpu.SemaphoreType.REGULAR((7,)),
            pltpu.SemaphoreType.REGULAR((COLUMNS,)),
            pltpu.SemaphoreType.REGULAR((COLUMNS,)),
        ],
        compiler_params=pltpu.CompilerParams(collective_id=0, has_side_effects=True, vmem_limit_bytes=56 * 2**20),
        cost_estimate=pl.CostEstimate(flops=2 * 16 * rows * rows * width, bytes_accessed=8 * rows * width, transcendentals=0),
    )(image_emb, text_emb, image_ids.reshape(1, rows), text_ids.reshape(1, rows))
    loss, image_grad, text_grad = pl.pallas_call(
        write_out,
        out_shape=tuple(jax.ShapeDtypeStruct(*s) for s in shapes),
        in_specs=[in_vmem] * 3,
        out_specs=(in_hbm, in_hbm, in_hbm),
        scratch_shapes=[pltpu.SemaphoreType.DMA((2 * PIECES + 1,))],
        compiler_params=pltpu.CompilerParams(vmem_limit_bytes=4 * 2**20),
    )(*results)
    return loss.reshape(rows), image_grad, text_grad


def solution(mesh):
    sizes = dict(mesh.shape)
    vector, matrix = P(("group", "blk")), P(("group", "blk"), None)
    return jax.shard_map(
        functools.partial(per_device, sizes["group"], sizes["blk"]), mesh=mesh,
        in_specs=(matrix, matrix, vector, vector), out_specs=(vector, matrix, matrix), check_vma=False)
```
